32 devices in a mesh: dp: 4 (over y, x), expert: 8 (over z, core).
Axes of the slice: x: 2, y: 2, z: 4, core: 2. Of those that a mesh axis runs over, the one named last changes fastest.
Arguments:
- output_grad: bfloat16 [6144, 2048], P(('dp', 'expert')), may hold values from -3 to 3
- routes: int32 [6144, 2], P(('dp', 'expert')), may hold values from 0 to 7, all different within a row; in each aligned block of 192 rows (0 to 191, 192 to 383, ...) at most 72 rows name the same one
- combine_weights: bfloat16 [6144, 2], P(('dp', 'expert')), may hold values from 0.049804688 to 0.5
- saved_hidden: bfloat16 [18432, 768], P(('dp', 'expert')), may hold values from -0.796875 to 0.796875
- down_weight: bfloat16 [8, 768, 2048], P('expert', 'dp'), may hold values from -0.21875 to 0.21875
Outputs:
- hidden_grad: bfloat16 [18432, 768], P(('dp', 'expert'))
- weight_grad: float32 [8, 768, 2048], P('expert', 'dp')
- route_grad: float32 [6144, 2], P(('dp', 'expert'))
The draws below stay inside these ranges and needn't reach their ends.
Inputs may be any that keep to these rules, and one draw needn't show every extreme that they name: Each token names 2 different experts; among the 192 rows of one device no expert is named by more than 72 routes.
All inputs are finite; a program needn't handle non-finite values.
Results may differ from the reference program's by a relative error of at most 0.008.
Values may be sent and summed in bfloat16 or wider, within the bound.
A program may use at most 64 MiB of HBM per device.

```python
import math
import jax
import jax.numpy as jnp
import numpy as np
from jax import lax

D_W = 2048
FF_W = 768
TOK_DEV = 192
TOPK = 2
EXPERTS = 8
CAP = 72
SLOTS = 576
TOKENS = 6144
N_DP = 4
N_EXPERT = 8
DEVICES = 32


def block_levels(stream_key, extent, split, least, largest):
    gain, own = 1.0, jax.random.fold_in(stream_key, 6)
    for dim, blocks in split:
        heights = jnp.exp(jax.random.uniform(jax.random.fold_in(own, dim), (blocks,), jnp.float32, least / len(split), largest / len(split)))
        gain = gain * jnp.repeat(heights, extent[dim] // blocks).reshape([-1 if axis == dim else 1 for axis in range(len(extent))])
    return gain


def assign_block(key, own, number, rows, count, top, bound, skew):
    sequence = jax.random.permutation(key, count)
    heavy_load, usual = shares(count, rows * top, bound, skew, True), shares(count, rows * top, bound, skew, False)
    places = jnp.arange(count)

    def named(lengths, offset_by):
        used = int((lengths > 0).sum())
        fixed = max(1, used // 4)
        shifted = fixed + (places - fixed + offset_by * (used - fixed)) % max(1, count - fixed)
        return jnp.zeros((count,), jnp.int32).at[sequence[jnp.where(places < fixed, places, shifted)]].set(jnp.asarray(lengths, jnp.int32))

    lengths = jnp.where(number % 4 == 0, named(heavy_load, number // 4), named(usual, number - number // 4 - 1))
    mixed = jax.random.permutation(jax.random.fold_in(own, 3), count)
    donor, sink = mixed[0:count // 2 * 2:2], mixed[1:count // 2 * 2:2]
    slack = jnp.minimum(lengths[donor] - 1, bound - lengths[sink]) // 2
    slack = jnp.where((donor == sequence[0]) | (sink == sequence[0]) | (lengths[sink] == 0), 0, jnp.maximum(slack, 0))
    shifted = jax.random.randint(jax.random.fold_in(own, 4), (count // 2,), 0, 1 << 20) % (slack + 1)
    lengths = lengths.at[donor].add(-shifted).at[sink].add(shifted)
    labels = jnp.searchsorted(jnp.cumsum(lengths), jnp.arange(rows * top), side="right").astype(jnp.int32)
    table = labels.reshape(top, rows).T
    table = table[jax.random.permutation(jax.random.fold_in(own, 1), rows)]
    offset_by = jax.random.randint(jax.random.fold_in(own, 2), (rows, 1), 0, top)
    return jnp.take_along_axis(table, (jnp.arange(top)[None, :] + offset_by) % top, axis=1)


def shares(number_of, total, limit, skew, full):
    weights = [(1 << 20) // math.isqrt(grade ** skew) + 1 for grade in range(1, number_of + 1)]
    largest = limit if full else min(limit, max(-(-total // number_of), total * weights[0] // sum(weights)))
    least = 1 if total - largest >= number_of - 1 else 0
    counts, spare = [largest] + [least] * (number_of - 1), total - largest - least * (number_of - 1)
    while spare > 0:
        movable = [i for i in range(1, number_of) if counts[i] < largest] or [i for i in range(1, number_of) if counts[i] < limit]
        whole, budget = sum([weights[i] for i in movable]), spare
        for i in movable:
            extra = min(limit - counts[i], max(1, budget * weights[i] // whole), spare)
            counts[i] = counts[i] + extra
            spare = spare - extra
    return np.array(counts)


def noise(own_key, extent, scale, bound, split=(), held_as=jnp.bfloat16):
    drawn = scale * jax.random.normal(own_key, extent, jnp.float32)
    if split:
        drawn = drawn * block_levels(own_key, extent, split, -0.22, 0.18)
    return jnp.clip(drawn, -bound, bound).astype(held_as)


def setup_inputs(seed: int = 0) -> dict:
    streams_of = jax.random.split(jax.random.key(seed), 6)
    output_grad = noise(streams_of[0], (TOKENS, D_W), 0.5, 3.0, ((0, 32),))
    routes_keys = jax.random.split(jax.random.fold_in(streams_of[1], 1), TOKENS // TOK_DEV)
    routes_turns = jax.random.permutation(jax.random.fold_in(streams_of[1], 3), TOKENS // TOK_DEV)
    routes = jax.vmap(lambda own, number: assign_block(jax.random.fold_in(streams_of[1], 2), own, number, TOK_DEV, EXPERTS, TOPK, CAP, 2))(routes_keys, routes_turns).reshape((TOKENS, TOPK))
    combine_weights = jnp.clip(jnp.exp(math.log(0.5) - 2.306499 * jax.random.uniform(streams_of[2], (TOKENS, TOPK), jnp.float32) ** block_levels(streams_of[2], (TOKENS, TOPK), ((0, 32),), -0.2, 0.2)), 0.049804688, 0.5).astype(jnp.bfloat16)
    saved_hidden = noise(streams_of[3], (DEVICES * SLOTS, FF_W), 0.1, 0.796875, ((0, 32),))
    down_weight = noise(streams_of[4], (EXPERTS, FF_W, D_W), FF_W ** -0.5, 0.21875, ((0, 8), (1, 4)))
    return dict(output_grad=output_grad, routes=routes, combine_weights=combine_weights, saved_hidden=saved_hidden, down_weight=down_weight)


def slot_positions(route_block):
    flat_ids = route_block.reshape(-1)
    one_hot = (flat_ids[:, None] == jnp.arange(EXPERTS, dtype=jnp.int32)[None, :]).astype(jnp.int32)
    earlier = jnp.cumsum(one_hot, axis=0) - one_hot
    return flat_ids, jnp.sum(earlier * one_hot, axis=1).astype(jnp.int32)


def reference(output_grad, routes, combine_weights, saved_hidden, down_weight):
    route_total = TOK_DEV * TOPK
    blocks = routes.reshape(DEVICES, route_total)
    expert_ids, positions = jax.vmap(slot_positions)(blocks)
    device_ids = jnp.arange(DEVICES, dtype=jnp.int32)[:, None]
    replica = device_ids // N_EXPERT
    sender = device_ids % N_EXPERT
    slot_index = ((replica * N_EXPERT + expert_ids) * SLOTS + sender * CAP + positions).reshape(-1).astype(jnp.int32)
    route_index = jnp.arange(DEVICES * route_total, dtype=jnp.int32)
    slot_owner = jnp.full((DEVICES * SLOTS,), DEVICES * route_total, jnp.int32).at[slot_index].set(route_index)
    flat_weights = combine_weights.reshape(-1)

    def one_device(device):
        picked = lax.dynamic_slice_in_dim(slot_owner, device * SLOTS, SLOTS)
        is_live = picked < DEVICES * route_total
        safe_index = jnp.where(is_live, picked, 0).astype(jnp.int32)
        grad_rows = jnp.where(is_live[:, None], output_grad[safe_index // TOPK], jnp.zeros((), jnp.bfloat16))
        slot_weights = jnp.where(is_live, flat_weights[safe_index], jnp.zeros((), jnp.bfloat16)).astype(jnp.float32)
        hidden = lax.dynamic_slice_in_dim(saved_hidden, device * SLOTS, SLOTS)
        expert = device % N_EXPERT
        matrix = lax.dynamic_index_in_dim(down_weight, expert, 0, keepdims=False)
        unscaled = lax.dot_general(grad_rows, matrix, (((1,), (1,)), ((), ())), preferred_element_type=jnp.float32)
        hidden_grad = (slot_weights[:, None] * unscaled).astype(jnp.bfloat16)
        recomputed = jnp.dot(hidden, matrix, preferred_element_type=jnp.float32)
        route_terms = jnp.sum(grad_rows.astype(jnp.float32) * recomputed, axis=1)
        weighted = (slot_weights[:, None] * grad_rows.astype(jnp.float32)).astype(jnp.bfloat16)
        partial_grad = lax.dot_general(hidden, weighted, (((0,), (0,)), ((), ())), preferred_element_type=jnp.float32)
        rounded = lax.optimization_barrier(partial_grad.astype(jnp.bfloat16)).astype(jnp.float32)
        return hidden_grad, route_terms, rounded

    def one_replica(running, replica_index):
        devices_here = replica_index * N_EXPERT + jnp.arange(N_EXPERT, dtype=jnp.int32)
        hidden_grads, route_terms, partials = lax.map(one_device, devices_here)
        return running + partials, (hidden_grads, route_terms)

    initial = jnp.zeros((EXPERTS, FF_W, D_W), jnp.float32)
    weight_grad, (hidden_grads, route_terms) = lax.scan(one_replica, initial, jnp.arange(N_DP, dtype=jnp.int32))
    hidden_grad = hidden_grads.reshape(DEVICES * SLOTS, FF_W)
    route_grad = route_terms.reshape(-1)[slot_index].reshape(TOKENS, TOPK)
    return hidden_grad, weight_grad, route_grad
```

```python
import jax
import jax.numpy as jnp
from jax import lax
from jax.sharding import PartitionSpec as P


def route_slots(routes, experts, capacity):
    flat_ids = routes.reshape(-1)
    place = jnp.arange(flat_ids.shape[0], dtype=jnp.int32)
    same = flat_ids[:, None] == flat_ids[None, :]
    rank = jnp.sum((same & (place[None, :] < place[:, None])).astype(jnp.int32), axis=1)
    return flat_ids * capacity + rank


def per_device(output_grad, routes, combine_weights, saved_hidden, down_weight):
    experts = lax.axis_size("expert")
    slot_count = saved_hidden.shape[0]
    capacity = slot_count // experts
    features = output_grad.shape[1]
    route_total = routes.shape[0] * routes.shape[1]
    target = route_slots(routes, experts, capacity)
    source = (
        jnp.full((slot_count,), route_total, jnp.int32)
        .at[target]
        .set(jnp.arange(route_total, dtype=jnp.int32))
    )
    is_live = source < route_total
    safe_index = jnp.where(is_live, source, 0)
    send_rows = jnp.where(
        is_live[:, None], output_grad[safe_index // routes.shape[1]], jnp.zeros((), jnp.bfloat16)
    )
    send_weights = jnp.where(
        is_live, combine_weights.reshape(-1)[safe_index], jnp.zeros((), jnp.bfloat16)
    )
    recv_rows, recv_weights = (
        lax.all_to_all(
            send_rows.reshape(experts, capacity, features),
            "expert",
            split_axis=0,
            concat_axis=0,
            tiled=True,
        ),
        lax.all_to_all(
            send_weights.reshape(experts, capacity),
            "expert",
            split_axis=0,
            concat_axis=0,
            tiled=True,
        ),
    )
    grad_rows = recv_rows.reshape(slot_count, features)
    slot_weights = recv_weights.reshape(slot_count).astype(jnp.float32)
    weighted = (slot_weights[:, None] * grad_rows.astype(jnp.float32)).astype(jnp.bfloat16)
    weight_shard = down_weight[0]
    contract = (((1,), (1,)), ((), ()))
    full_weight = lax.all_gather(weight_shard, "dp", axis=0, tiled=True)
    unscaled = lax.dot_general(grad_rows, full_weight, contract, preferred_element_type=jnp.float32)
    route_terms = jnp.sum(saved_hidden.astype(jnp.float32) * unscaled, axis=1)
    hidden_grad = (slot_weights[:, None] * unscaled).astype(jnp.bfloat16)
    grad_part = lax.psum_scatter(
        lax.dot_general(
            saved_hidden, weighted, (((0,), (0,)), ((), ())), preferred_element_type=jnp.float32
        ).astype(jnp.bfloat16),
        "dp",
        scatter_dimension=0,
        tiled=True,
    ).astype(jnp.float32)
    returned = lax.all_to_all(
        route_terms.reshape(experts, capacity), "expert", split_axis=0, concat_axis=0, tiled=True
    )
    route_grad = returned.reshape(-1)[target].reshape(routes.shape)
    return (hidden_grad, grad_part[None], route_grad)


def solution(mesh):
    return jax.shard_map(
        per_device,
        mesh=mesh,
        in_specs=(
            P(("dp", "expert"), None),
            P(("dp", "expert"), None),
            P(("dp", "expert"), None),
            P(("dp", "expert"), None),
            P("expert", "dp", None),
        ),
        out_specs=(P(("dp", "expert"), None), P("expert", "dp", None), P(("dp", "expert"), None)),
        check_vma=False,
    )
```

```python
import functools

import jax
import jax.numpy as jnp
from jax import lax
from jax.experimental import pallas as pl
from jax.experimental.pallas import tpu as pltpu
from jax.sharding import PartitionSpec as P

MESH = pl.DeviceIdType.MESH
F32 = jnp.float32
BF16 = jnp.bfloat16
LANES = 128


def kernel(
    n_dp, n_ex, chunks,
    grad_ref, routes_ref, weights_ref, hidden_ref, shard_ref,
    hgrad_ref, wgrad_ref, rgrad_ref,
    pick, send, recv, full, scale_out, scale_in, term_out, term_in,
    hid, unscaled, part, landed,
    row_s, row_r, mat_s, mat_r, sca_s, sca_r, ter_s, ter_r, red_s, red_r,
):
    dp, ex = lax.axis_index("dp"), lax.axis_index("expert")
    cap = hidden_ref.shape[1]
    wide = send.shape[2]
    fc = send.shape[3]
    depth = shard_ref.shape[0]
    tokens = grad_ref.shape[0]
    ff = hidden_ref.shape[2]

    def columns(c):
        return pl.ds(pl.multiple_of(c * fc, fc), fc)

    def mat_copy(c, k):
        to = lax.rem(dp + k, n_dp)
        return pltpu.make_async_remote_copy(
            src_ref=shard_ref.at[:, columns(c)], dst_ref=full.at[c, dp],
            send_sem=mat_s.at[c, to], recv_sem=mat_r.at[c, dp],
            device_id=(to, ex), device_id_type=MESH)

    def mat_arrival(c, k):
        src = lax.rem(dp + k, n_dp)
        return pltpu.make_async_remote_copy(
            src_ref=shard_ref.at[:, columns(c)], dst_ref=full.at[c, src],
            send_sem=mat_s.at[c, src], recv_sem=mat_r.at[c, src],
            device_id=(src, ex), device_id_type=MESH)

    def row_copy(c, k):
        to = lax.rem(ex + k, n_ex)
        return pltpu.make_async_remote_copy(
            src_ref=send.at[c, to], dst_ref=recv.at[c, ex],
            send_sem=row_s.at[c, to], recv_sem=row_r.at[c, ex],
            device_id=(dp, to), device_id_type=MESH)

    def row_arrival(c, k):
        src = lax.rem(ex + k, n_ex)
        return pltpu.make_async_remote_copy(
            src_ref=send.at[c, src], dst_ref=recv.at[c, src],
            send_sem=row_s.at[c, src], recv_sem=row_r.at[c, src],
            device_id=(dp, src), device_id_type=MESH)

    def red_copy(c, k):
        to = lax.rem(dp + k, n_dp)
        return pltpu.make_async_remote_copy(
            src_ref=part.at[c, to], dst_ref=landed.at[c, dp],
            send_sem=red_s.at[c, to], recv_sem=red_r.at[c, dp],
            device_id=(to, ex), device_id_type=MESH)

    def red_arrival(c, k):
        src = lax.rem(dp + k, n_dp)
        return pltpu.make_async_remote_copy(
            src_ref=part.at[c, src], dst_ref=landed.at[c, src],
            send_sem=red_s.at[c, src], recv_sem=red_r.at[c, src],
            device_id=(src, ex), device_id_type=MESH)

    def small_copy(out, into, s, r, k):
        to = lax.rem(ex + k, n_ex)
        return pltpu.make_async_remote_copy(
            src_ref=out.at[to], dst_ref=into.at[ex],
            send_sem=s.at[to], recv_sem=r.at[ex],
            device_id=(dp, to), device_id_type=MESH)

    def small_arrival(out, into, s, r, k):
        src = lax.rem(ex + k, n_ex)
        return pltpu.make_async_remote_copy(
            src_ref=out.at[src], dst_ref=into.at[src],
            send_sem=s.at[src], recv_sem=r.at[src],
            device_id=(dp, src), device_id_type=MESH)

    def each(low, high, body):
        def step(i, carry):
            body(i)
            return carry
        lax.fori_loop(low, high, step, 0)

    barrier = pltpu.get_barrier_semaphore()
    each(1, n_dp, lambda k: pl.semaphore_signal(
        barrier, inc=1, device_id=(lax.rem(dp + k, n_dp), ex), device_id_type=MESH))
    each(1, n_ex, lambda k: pl.semaphore_signal(
        barrier, inc=1, device_id=(dp, lax.rem(ex + k, n_ex)), device_id_type=MESH))

    first, second = routes_ref[0:1, :], routes_ref[1:2, :]
    names = lax.broadcasted_iota(jnp.int32, (n_ex, tokens), 0)
    named = (names == first) | (names == second)
    earlier = (lax.broadcasted_iota(jnp.int32, (tokens, tokens), 0)
               < lax.broadcasted_iota(jnp.int32, (tokens, tokens), 1))
    rank = jnp.dot(jnp.where(named, 1.0, 0.0).astype(BF16),
                   jnp.where(earlier, 1.0, 0.0).astype(BF16), preferred_element_type=F32)
    rank = jnp.where(named, rank.astype(jnp.int32), -1)
    scale_of = (jnp.where(names == first, weights_ref[0:1, :], 0.0)
                + jnp.where(names == second, weights_ref[1:2, :], 0.0))
    place = lax.broadcasted_iota(jnp.int32, (wide, tokens), 0)
    diagonal = (lax.broadcasted_iota(jnp.int32, (wide, LANES), 0)
                == lax.broadcasted_iota(jnp.int32, (wide, LANES), 1))
    for e in range(n_ex):
        chosen = place == rank[e:e + 1, :]
        pick[e * wide:(e + 1) * wide, :] = jnp.where(chosen, 1.0, 0.0).astype(BF16)
        column = jnp.sum(jnp.where(chosen, scale_of[e:e + 1, :], 0.0), axis=1, keepdims=True)
        row = jnp.sum(jnp.where(diagonal, column, 0.0), axis=0, keepdims=True)
        scale_out[e] = jnp.broadcast_to(row, (8, LANES))

    pl.semaphore_wait(barrier, n_dp + n_ex - 2)
    each(1, n_ex, lambda k: small_copy(scale_out, scale_in, sca_s, sca_r, k).start())
    scale_in[ex] = scale_out[ex]

    def dispatch(c):
        rows = jnp.dot(pick[...], grad_ref[:, columns(c)], preferred_element_type=F32)
        send[c] = rows.astype(BF16).reshape(n_ex, wide, fc)
        each(1, n_ex, lambda k: row_copy(c, k).start())
        each(1, n_dp, lambda k: mat_copy(c, k).start())
        recv[c, ex] = send[c, ex]
        full[c, dp] = shard_ref[:, columns(c)]
    each(0, chunks, dispatch)

    padded = jnp.concatenate(
        [hidden_ref[...].astype(F32), jnp.zeros((n_ex, wide - cap, ff), F32)], axis=1)
    hid[...] = padded.reshape(n_ex * wide, ff).T.astype(BF16)

    each(1, n_ex, lambda k: small_arrival(scale_out, scale_in, sca_s, sca_r, k).wait())

    def scale_column():
        return jnp.concatenate(
            [jnp.sum(jnp.where(diagonal, scale_in[j, 0:1, :], 0.0), axis=1, keepdims=True)
             for j in range(n_ex)], axis=0)

    def work(c):
        each(1, n_ex, lambda k: row_arrival(c, k).wait())
        rows = recv[c].reshape(n_ex * wide, fc)
        weighted = (scale_column() * rows.astype(F32)).astype(BF16)
        share = jnp.dot(hid[...], weighted, preferred_element_type=F32)
        part[c] = share.astype(BF16).reshape(n_dp, depth, fc)
        each(1, n_dp, lambda k: red_copy(c, k).start())
        landed[c, dp] = part[c, dp]
        each(1, n_dp, lambda k: mat_arrival(c, k).wait())
        product = lax.dot_general(
            rows, full[c].reshape(n_dp * depth, fc), (((1,), (1,)), ((), ())),
            preferred_element_type=F32)

        @pl.when(c == 0)
        def _():
            unscaled[...] = product

        @pl.when(c > 0)
        def _():
            unscaled[...] += product
    each(0, chunks, work)

    for j in range(n_ex):
        block = unscaled[j * wide:j * wide + cap, :]
        term = jnp.sum(hidden_ref[j].astype(F32) * block, axis=1, keepdims=True)
        row = jnp.sum(jnp.where(diagonal[0:cap], term, 0.0), axis=0, keepdims=True)
        term_out[j] = jnp.broadcast_to(row, (8, LANES))
    each(1, n_ex, lambda k: small_copy(term_out, term_in, ter_s, ter_r, k).start())
    term_in[ex] = term_out[ex]
    for j in range(n_ex):
        column = jnp.sum(jnp.where(diagonal, scale_in[j, 0:1, :], 0.0), axis=1, keepdims=True)
        hgrad_ref[j] = (column[0:cap] * unscaled[j * wide:j * wide + cap, :]).astype(BF16)

    def reduce(c):
        each(1, n_dp, lambda k: red_arrival(c, k).wait())
        wgrad_ref[:, columns(c)] = jnp.sum(landed[c].astype(F32), axis=0)
    each(0, chunks, reduce)

    each(1, n_ex, lambda k: small_arrival(term_out, term_in, ter_s, ter_r, k).wait())
    first_out = jnp.zeros((1, tokens), F32)
    second_out = jnp.zeros((1, tokens), F32)
    for e in range(n_ex):
        column = jnp.sum(jnp.where(diagonal, term_in[e, 0:1, :], 0.0), axis=1, keepdims=True)
        back = jnp.sum(jnp.where(place == rank[e:e + 1, :], column, 0.0), axis=0, keepdims=True)
        first_out += jnp.where(first == e, back, 0.0)
        second_out += jnp.where(second == e, back, 0.0)
    rgrad_ref[0:1, :] = first_out
    rgrad_ref[1:2, :] = second_out


def per_device(output_grad, routes, combine_weights, saved_hidden, down_weight):
    n_dp, n_ex = lax.axis_size("dp"), lax.axis_size("expert")
    tokens, features = output_grad.shape
    slots, ff = saved_hidden.shape
    cap = slots // n_ex
    wide = -(-cap // 16) * 16
    depth = down_weight.shape[1]
    chunks = 4
    fc = features // chunks
    dma = pltpu.SemaphoreType.DMA
    hgrad, wgrad, rgrad = pl.pallas_call(
        functools.partial(kernel, n_dp, n_ex, chunks),
        out_shape=(
            jax.ShapeDtypeStruct((n_ex, cap, ff), BF16),
            jax.ShapeDtypeStruct((depth, features), F32),
            jax.ShapeDtypeStruct((2, tokens), F32),
        ),
        in_specs=[pl.BlockSpec(memory_space=pltpu.VMEM)] * 5,
        out_specs=[pl.BlockSpec(memory_space=pltpu.VMEM)] * 3,
        scratch_shapes=[
            pltpu.VMEM((n_ex * wide, tokens), BF16),
            pltpu.VMEM((chunks, n_ex, wide, fc), BF16),
            pltpu.VMEM((chunks, n_ex, wide, fc), BF16),
            pltpu.VMEM((chunks, n_dp, depth, fc), BF16),
            pltpu.VMEM((n_ex, 8, LANES), F32),
            pltpu.VMEM((n_ex, 8, LANES), F32),
            pltpu.VMEM((n_ex, 8, LANES), F32),
            pltpu.VMEM((n_ex, 8, LANES), F32),
            pltpu.VMEM((ff, n_ex * wide), BF16),
            pltpu.VMEM((n_ex * wide, ff), F32),
            pltpu.VMEM((chunks, n_dp, depth, fc), BF16),
            pltpu.VMEM((chunks, n_dp, depth, fc), BF16),
            dma((chunks, n_ex)), dma((chunks, n_ex)),
            dma((chunks, n_dp)), dma((chunks, n_dp)),
            dma((n_ex,)), dma((n_ex,)), dma((n_ex,)), dma((n_ex,)),
            dma((chunks, n_dp)), dma((chunks, n_dp)),
        ],
        compiler_params=pltpu.CompilerParams(
            collective_id=0, has_side_effects=True, vmem_limit_bytes=52 * 2**20
        ),
        cost_estimate=pl.CostEstimate(
            flops=4 * slots * features * ff, bytes_accessed=8 * 2**20, transcendentals=0),
    )(
        output_grad, routes.T, combine_weights.T.astype(F32),
        saved_hidden.reshape(n_ex, cap, ff), down_weight[0],
    )
    return hgrad.reshape(slots, ff), wgrad[None], rgrad.T


def solution(mesh):
    return jax.shard_map(
        per_device,
        mesh=mesh,
        in_specs=(
            P(("dp", "expert"), None),
            P(("dp", "expert"), None),
            P(("dp", "expert"), None),
            P(("dp", "expert"), None),
            P("expert", "dp", None),
        ),
        out_specs=(P(("dp", "expert"), None), P("expert", "dp", None), P(("dp", "expert"), None)),
        check_vma=False,
    )
```

```python
import functools

import jax
import jax.numpy as jnp
from jax import lax
from jax.experimental import pallas as pl
from jax.experimental.pallas import tpu as pltpu
from jax.sharding import PartitionSpec as P

MESH = pl.DeviceIdType.MESH
F32 = jnp.float32
BF16 = jnp.bfloat16
LANES = 128


def kernel(
    n_dp, n_ex, chunks,
    grad_ref, routes_ref, weights_ref, hidden_ref, shard_ref,
    hgrad_ref, wgrad_ref, rgrad_ref,
    pick, send, recv, full, scale_out, scale_in, term_out, term_in,
    hid, unscaled, part, landed,
    row_s, row_r, mat_s, mat_r, sca_s, sca_r, ter_s, ter_r, red_s, red_r,
):
    dp, ex = lax.axis_index("dp"), lax.axis_index("expert")
    cap = hidden_ref.shape[1]
    wide = send.shape[2] // 2
    sub = send.shape[3]
    fc = 2 * sub
    depth = shard_ref.shape[0]
    tokens = grad_ref.shape[0]
    ff = hidden_ref.shape[2]

    def columns(c):
        return pl.ds(pl.multiple_of(c * fc, fc), fc)

    def dp_copy(src, dst, s, r, to):
        return pltpu.make_async_remote_copy(
            src_ref=src, dst_ref=dst, send_sem=s, recv_sem=r,
            device_id=(to, ex), device_id_type=MESH)

    def narrow(t):
        return pl.ds(pl.multiple_of(t * sub, sub), sub)

    square = n_dp == 4
    across = dp + 1 - 2 * lax.rem(dp, 2)
    along = lax.rem(dp + 2, n_dp)
    corner = lax.rem(across + 2, n_dp)
    near = (across, along)

    def mat_copy(t, to):
        return dp_copy(shard_ref.at[:, narrow(t)], full.at[t, dp], mat_s.at[t, to], mat_r.at[t, dp], to)

    def mat_pass(t, h):
        return dp_copy(full.at[t, near[h]], full.at[t, near[h]], mat_s.at[t, corner],
                       mat_r.at[t, near[h]], near[1 - h])

    def mat_arrival(t, src):
        return dp_copy(shard_ref.at[:, narrow(t)], full.at[t, src], mat_s.at[t, src], mat_r.at[t, src], src)

    def mat_start(t):
        if square:
            mat_copy(t, across).start()
            mat_copy(t, along).start()
        else:
            each(1, n_dp, lambda k: mat_copy(t, lax.rem(dp + k, n_dp)).start())

    def mat_forward(t, h):
        if square:
            mat_arrival(t, near[h]).wait_recv()
            mat_pass(t, h).start()

    def mat_wait(t, h):
        if square:
            mat_arrival(t, near[1 - h]).wait_recv()
            mat_arrival(t, corner).wait()
            mat_arrival(t, across).wait_send()
            mat_arrival(t, along).wait_send()
        else:
            each(1, n_dp, lambda k: mat_arrival(t, lax.rem(dp + k, n_dp)).wait())

    def red_copy(t, block, slot, to):
        return dp_copy(part.at[t, block], landed.at[t, slot], red_s.at[t, slot], red_r.at[t, slot], to)

    def red_far(t, k):
        to = lax.rem(dp + k, n_dp)
        return dp_copy(part.at[t, to], landed.at[t, dp], red_s.at[t, to], red_r.at[t, dp], to)

    def red_far_arrival(t, k):
        src = lax.rem(dp + k, n_dp)
        return dp_copy(part.at[t, src], landed.at[t, src], red_s.at[t, src], red_r.at[t, src], src)

    def red_start(t, h):
        if square:
            red_copy(t, corner, 1, near[h]).start()
            red_copy(t, near[h], 0, near[h]).start()
        else:
            each(1, n_dp, lambda k: red_far(t, k).start())

    def red_forward(t, h):
        if square:
            red_copy(t, corner, 1, near[h]).wait()
            total = part[t, near[1 - h]].astype(F32) + landed[t, 1].astype(F32)
            part[t, near[1 - h]] = total.astype(BF16)
            red_copy(t, near[1 - h], 2, near[1 - h]).start()

    def red_finish(t, h):
        if square:
            red_copy(t, near[h], 0, near[h]).wait()
            red_copy(t, near[1 - h], 2, near[1 - h]).wait()
            return part[t, dp].astype(F32) + landed[t, 0].astype(F32) + landed[t, 2].astype(F32)
        each(1, n_dp, lambda k: red_far_arrival(t, k).wait())
        landed[t, dp] = part[t, dp]
        return jnp.sum(landed[t].astype(F32), axis=0)

    def row_copy(c, k):
        to = lax.rem(ex + k, n_ex)
        return pltpu.make_async_remote_copy(
            src_ref=send.at[c, to], dst_ref=recv.at[c, ex],
            send_sem=row_s.at[c, to], recv_sem=row_r.at[c, ex],
            device_id=(dp, to), device_id_type=MESH)

    def row_arrival(c, k):
        src = lax.rem(ex + k, n_ex)
        return pltpu.make_async_remote_copy(
            src_ref=send.at[c, src], dst_ref=recv.at[c, src],
            send_sem=row_s.at[c, src], recv_sem=row_r.at[c, src],
            device_id=(dp, src), device_id_type=MESH)

    def small_copy(out, into, s, r, k):
        to = lax.rem(ex + k, n_ex)
        return pltpu.make_async_remote_copy(
            src_ref=out.at[to], dst_ref=into.at[ex],
            send_sem=s.at[to], recv_sem=r.at[ex],
            device_id=(dp, to), device_id_type=MESH)

    def small_arrival(out, into, s, r, k):
        src = lax.rem(ex + k, n_ex)
        return pltpu.make_async_remote_copy(
            src_ref=out.at[src], dst_ref=into.at[src],
            send_sem=s.at[src], recv_sem=r.at[src],
            device_id=(dp, src), device_id_type=MESH)

    def each(low, high, body):
        def step(i, carry):
            body(i)
            return carry
        lax.fori_loop(low, high, step, 0)

    barrier = pltpu.get_barrier_semaphore()
    each(1, n_dp, lambda k: pl.semaphore_signal(
        barrier, inc=1, device_id=(lax.rem(dp + k, n_dp), ex), device_id_type=MESH))
    each(1, n_ex, lambda k: pl.semaphore_signal(
        barrier, inc=1, device_id=(dp, lax.rem(ex + k, n_ex)), device_id_type=MESH))

    first, second = routes_ref[0:1, :], routes_ref[1:2, :]
    names = lax.broadcasted_iota(jnp.int32, (n_ex, tokens), 0)
    named = (names == first) | (names == second)
    earlier = (lax.broadcasted_iota(jnp.int32, (tokens, tokens), 0)
               < lax.broadcasted_iota(jnp.int32, (tokens, tokens), 1))
    rank = jnp.dot(jnp.where(named, 1.0, 0.0).astype(BF16),
                   jnp.where(earlier, 1.0, 0.0).astype(BF16), preferred_element_type=F32)
    rank = jnp.where(named, rank.astype(jnp.int32), -1)
    scale_of = (jnp.where(names == first, weights_ref[0:1, :], 0.0)
                + jnp.where(names == second, weights_ref[1:2, :], 0.0))
    place = lax.broadcasted_iota(jnp.int32, (wide, tokens), 0)
    diagonal = (lax.broadcasted_iota(jnp.int32, (wide, LANES), 0)
                == lax.broadcasted_iota(jnp.int32, (wide, LANES), 1))
    picked = []
    for e in range(n_ex):
        chosen = place == rank[e:e + 1, :]
        picked.append(jnp.where(chosen, 1.0, 0.0))
        column = jnp.sum(jnp.where(chosen, scale_of[e:e + 1, :], 0.0), axis=1, keepdims=True)
        row = jnp.sum(jnp.where(diagonal, column, 0.0), axis=0, keepdims=True)
        scale_out[e] = jnp.broadcast_to(row, (8, LANES))

    pick[...] = jnp.concatenate(picked, axis=0).astype(BF16)
    pl.semaphore_wait(barrier, n_dp + n_ex - 2)
    each(1, n_ex, lambda k: small_copy(scale_out, scale_in, sca_s, sca_r, k).start())
    scale_in[ex] = scale_out[ex]

    def dispatch(c):
        rows = jnp.dot(pick[...], grad_ref[:, columns(c)], preferred_element_type=F32)
        send[c] = jnp.concatenate(
            [rows[:, :sub].reshape(n_ex, wide, sub), rows[:, sub:].reshape(n_ex, wide, sub)],
            axis=1).astype(BF16)
        each(1, n_ex, lambda k: row_copy(c, k).start())
        recv[c, ex] = send[c, ex]
        for h in range(2):
            mat_start(2 * c + h)
            full[2 * c + h, dp] = shard_ref[:, narrow(2 * c + h)]
    each(0, chunks, dispatch)

    padded = hidden_ref[...].astype(F32)
    if wide > cap:
        padded = jnp.concatenate([padded, jnp.zeros((n_ex, wide - cap, ff), F32)], axis=1)
    hid[...] = padded.reshape(n_ex * wide, ff).T.astype(BF16)

    each(1, n_ex, lambda k: small_arrival(scale_out, scale_in, sca_s, sca_r, k).wait())

    def scale_column():
        return jnp.concatenate(
            [jnp.sum(jnp.where(diagonal, scale_in[j, 0:1, :], 0.0), axis=1, keepdims=True)
             for j in range(n_ex)], axis=0)

    def pass_on(c):
        for h in range(2):
            mat_forward(2 * c + h, h)
    each(0, chunks, pass_on)

    def work(c):
        each(1, n_ex, lambda k: row_arrival(c, k).wait())
        both = recv[c].astype(F32)
        halves = [both[:, h * wide:(h + 1) * wide].reshape(n_ex * wide, sub) for h in range(2)]
        for h in range(2):
            weighted = (scale_column() * halves[h]).astype(BF16)
            share = jnp.dot(hid[...], weighted, preferred_element_type=F32)
            part[2 * c + h] = share.astype(BF16).reshape(n_dp, depth, sub)
            red_start(2 * c + h, h)
        product = jnp.zeros(unscaled.shape, F32)
        for h in range(2):
            mat_wait(2 * c + h, h)
            product += lax.dot_general(
                halves[h].astype(BF16), full[2 * c + h].reshape(n_dp * depth, sub),
                (((1,), (1,)), ((), ())), preferred_element_type=F32)

        @pl.when(c == 0)
        def _():
            unscaled[...] = product

        @pl.when(c > 0)
        def _():
            unscaled[...] += product
            for h in range(2):
                red_forward(2 * (c - 1) + h, h)
    each(0, chunks, work)

    for j in range(n_ex):
        block = unscaled[j * wide:j * wide + cap, :]
        term = jnp.sum(hidden_ref[j].astype(F32) * block, axis=1, keepdims=True)
        row = jnp.sum(jnp.where(diagonal[0:cap], term, 0.0), axis=0, keepdims=True)
        term_out[j] = jnp.broadcast_to(row, (8, LANES))
    each(1, n_ex, lambda k: small_copy(term_out, term_in, ter_s, ter_r, k).start())
    term_in[ex] = term_out[ex]
    for j in range(n_ex):
        column = jnp.sum(jnp.where(diagonal, scale_in[j, 0:1, :], 0.0), axis=1, keepdims=True)
        hgrad_ref[j] = (column[0:cap] * unscaled[j * wide:j * wide + cap, :]).astype(BF16)

    for h in range(2):
        red_forward(2 * (chunks - 1) + h, h)

    def reduce(c):
        for h in range(2):
            wgrad_ref[:, narrow(2 * c + h)] = red_finish(2 * c + h, h)
    each(0, chunks, reduce)

    each(1, n_ex, lambda k: small_arrival(term_out, term_in, ter_s, ter_r, k).wait())
    first_out = jnp.zeros((1, tokens), F32)
    second_out = jnp.zeros((1, tokens), F32)
    for e in range(n_ex):
        column = jnp.sum(jnp.where(diagonal, term_in[e, 0:1, :], 0.0), axis=1, keepdims=True)
        back = jnp.sum(jnp.where(place == rank[e:e + 1, :], column, 0.0), axis=0, keepdims=True)
        first_out += jnp.where(first == e, back, 0.0)
        second_out += jnp.where(second == e, back, 0.0)
    rgrad_ref[0:1, :] = first_out
    rgrad_ref[1:2, :] = second_out


def per_device(output_grad, routes, combine_weights, saved_hidden, down_weight):
    n_dp, n_ex = lax.axis_size("dp"), lax.axis_size("expert")
    tokens, features = output_grad.shape
    slots, ff = saved_hidden.shape
    cap = slots // n_ex
    wide = -(-cap // 8) * 8
    depth = down_weight.shape[1]
    chunks = 4
    sub = features // (2 * chunks)
    dma = pltpu.SemaphoreType.DMA
    hgrad, wgrad, rgrad = pl.pallas_call(
        functools.partial(kernel, n_dp, n_ex, chunks),
        out_shape=(
            jax.ShapeDtypeStruct((n_ex, cap, ff), BF16),
            jax.ShapeDtypeStruct((depth, features), F32),
            jax.ShapeDtypeStruct((2, tokens), F32),
        ),
        in_specs=[pl.BlockSpec(memory_space=pltpu.VMEM)] * 5,
        out_specs=[pl.BlockSpec(memory_space=pltpu.VMEM)] * 3,
        scratch_shapes=[
            pltpu.VMEM((n_ex * wide, tokens), BF16),
            pltpu.VMEM((chunks, n_ex, 2 * wide, sub), BF16),
            pltpu.VMEM((chunks, n_ex, 2 * wide, sub), BF16),
            pltpu.VMEM((2 * chunks, n_dp, depth, sub), BF16),
            pltpu.VMEM((n_ex, 8, LANES), F32),
            pltpu.VMEM((n_ex, 8, LANES), F32),
            pltpu.VMEM((n_ex, 8, LANES), F32),
            pltpu.VMEM((n_ex, 8, LANES), F32),
            pltpu.VMEM((ff, n_ex * wide), BF16),
            pltpu.VMEM((n_ex * wide, ff), F32),
            pltpu.VMEM((2 * chunks, n_dp, depth, sub), BF16),
            pltpu.VMEM((2 * chunks, n_dp, depth, sub), BF16),
            dma((chunks, n_ex)), dma((chunks, n_ex)),
            dma((2 * chunks, n_dp)), dma((2 * chunks, n_dp)),
            dma((n_ex,)), dma((n_ex,)), dma((n_ex,)), dma((n_ex,)),
            dma((2 * chunks, n_dp)), dma((2 * chunks, n_dp)),
        ],
        compiler_params=pltpu.CompilerParams(
            collective_id=0, has_side_effects=True, vmem_limit_bytes=36 * 2**20
        ),
        cost_estimate=pl.CostEstimate(
            flops=4 * slots * features * ff, bytes_accessed=8 * 2**20, transcendentals=0),
    )(
        output_grad, routes.T, combine_weights.T.astype(F32),
        saved_hidden.reshape(n_ex, cap, ff), down_weight[0],
    )
    return hgrad.reshape(slots, ff), wgrad[None], rgrad.T


def solution(mesh):
    return jax.shard_map(
        per_device,
        mesh=mesh,
        in_specs=(
            P(("dp", "expert"), None),
            P(("dp", "expert"), None),
            P(("dp", "expert"), None),
            P(("dp", "expert"), None),
            P("expert", "dp", None),
        ),
        out_specs=(P(("dp", "expert"), None), P("expert", "dp", None), P(("dp", "expert"), None)),
        check_vma=False,
    )
```

```python
import functools

import jax
import jax.numpy as jnp
from jax import lax
from jax.experimental import pallas as pl
from jax.experimental.pallas import tpu as pltpu
from jax.sharding import PartitionSpec as P

MESH = pl.DeviceIdType.MESH
F32 = jnp.float32
BF16 = jnp.bfloat16
LANES = 128


def kernel(
    n_dp, n_ex, chunks,
    grad_ref, routes_ref, weights_ref, hidden_ref, shard_ref,
    hgrad_ref, wgrad_ref, rgrad_ref,
    pick, send, recv, full, scale_out, scale_in, term_out, term_in,
    hid, unscaled, part, landed,
    row_s, row_r, mat_s, mat_r, sca_s, sca_r, ter_s, ter_r, red_s, red_r,
):
    dp, ex = lax.axis_index("dp"), lax.axis_index("expert")
    cap = hidden_ref.shape[1]
    wide = send.shape[2] // 2
    sub = send.shape[3]
    fc = 2 * sub
    depth = shard_ref.shape[0]
    tokens = grad_ref.shape[0]
    ff = hidden_ref.shape[2]

    def columns(c):
        return pl.ds(pl.multiple_of(c * fc, fc), fc)

    def dp_copy(src, dst, s, r, to):
        return pltpu.make_async_remote_copy(
            src_ref=src, dst_ref=dst, send_sem=s, recv_sem=r,
            device_id=(to, ex), device_id_type=MESH)

    def narrow(t):
        return pl.ds(pl.multiple_of(t * sub, sub), sub)

    square = n_dp == 4
    across = dp + 1 - 2 * lax.rem(dp, 2)
    along = lax.rem(dp + 2, n_dp)
    corner = lax.rem(across + 2, n_dp)
    near = (across, along)

    def mat_copy(t, to):
        return dp_copy(shard_ref.at[:, narrow(t)], full.at[t, dp], mat_s.at[t, to], mat_r.at[t, dp], to)

    def mat_pass(t, h):
        return dp_copy(full.at[t, near[h]], full.at[t, near[h]], mat_s.at[t, corner],
                       mat_r.at[t, near[h]], near[1 - h])

    def mat_arrival(t, src):
        return dp_copy(shard_ref.at[:, narrow(t)], full.at[t, src], mat_s.at[t, src], mat_r.at[t, src], src)

    def mat_start(t):
        if square:
            mat_copy(t, across).start()
            mat_copy(t, along).start()
        else:
            each(1, n_dp, lambda k: mat_copy(t, lax.rem(dp + k, n_dp)).start())

    def mat_forward(t, h):
        if square:
            mat_arrival(t, near[h]).wait_recv()
            mat_pass(t, h).start()

    def mat_wait(t, h):
        if square:
            mat_arrival(t, near[1 - h]).wait_recv()
            mat_arrival(t, corner).wait()
            mat_arrival(t, across).wait_send()
            mat_arrival(t, along).wait_send()
        else:
            each(1, n_dp, lambda k: mat_arrival(t, lax.rem(dp + k, n_dp)).wait())

    def red_copy(t, block, slot, to):
        return dp_copy(part.at[t, block], landed.at[t, slot], red_s.at[t, slot], red_r.at[t, slot], to)

    def red_far(t, k):
        to = lax.rem(dp + k, n_dp)
        return dp_copy(part.at[t, to], landed.at[t, dp], red_s.at[t, to], red_r.at[t, dp], to)

    def red_far_arrival(t, k):
        src = lax.rem(dp + k, n_dp)
        return dp_copy(part.at[t, src], landed.at[t, src], red_s.at[t, src], red_r.at[t, src], src)

    def red_start(t, h):
        if square:
            red_copy(t, corner, 1, near[h]).start()
            red_copy(t, near[h], 0, near[h]).start()
        else:
            each(1, n_dp, lambda k: red_far(t, k).start())

    def red_forward(t, h):
        if square:
            red_copy(t, corner, 1, near[h]).wait()
            total = part[t, near[1 - h]].astype(F32) + landed[t, 1].astype(F32)
            part[t, near[1 - h]] = total.astype(BF16)
            red_copy(t, near[1 - h], 2, near[1 - h]).start()

    def red_finish(t, h):
        if square:
            red_copy(t, near[h], 0, near[h]).wait()
            red_copy(t, near[1 - h], 2, near[1 - h]).wait()
            return part[t, dp].astype(F32) + landed[t, 0].astype(F32) + landed[t, 2].astype(F32)
        each(1, n_dp, lambda k: red_far_arrival(t, k).wait())
        landed[t, dp] = part[t, dp]
        return jnp.sum(landed[t].astype(F32), axis=0)

    def row_copy(c, k):
        to = lax.rem(ex + k, n_ex)
        return pltpu.make_async_remote_copy(
            src_ref=send.at[c, to], dst_ref=recv.at[c, ex],
            send_sem=row_s.at[c, to], recv_sem=row_r.at[c, ex],
            device_id=(dp, to), device_id_type=MESH)

    def row_arrival(c, k):
        src = lax.rem(ex + k, n_ex)
        return pltpu.make_async_remote_copy(
            src_ref=send.at[c, src], dst_ref=recv.at[c, src],
            send_sem=row_s.at[c, src], recv_sem=row_r.at[c, src],
            device_id=(dp, src), device_id_type=MESH)

    def small_copy(out, into, s, r, k):
        to = lax.rem(ex + k, n_ex)
        return pltpu.make_async_remote_copy(
            src_ref=out.at[to], dst_ref=into.at[ex],
            send_sem=s.at[to], recv_sem=r.at[ex],
            device_id=(dp, to), device_id_type=MESH)

    def small_arrival(out, into, s, r, k):
        src = lax.rem(ex + k, n_ex)
        return pltpu.make_async_remote_copy(
            src_ref=out.at[src], dst_ref=into.at[src],
            send_sem=s.at[src], recv_sem=r.at[src],
            device_id=(dp, src), device_id_type=MESH)

    def each(low, high, body):
        def step(i, carry):
            body(i)
            return carry
        lax.fori_loop(low, high, step, 0)

    barrier = pltpu.get_barrier_semaphore()
    each(1, n_dp, lambda k: pl.semaphore_signal(
        barrier, inc=1, device_id=(lax.rem(dp + k, n_dp), ex), device_id_type=MESH))
    each(1, n_ex, lambda k: pl.semaphore_signal(
        barrier, inc=1, device_id=(dp, lax.rem(ex + k, n_ex)), device_id_type=MESH))

    first, second = routes_ref[0:1, :], routes_ref[1:2, :]
    names = lax.broadcasted_iota(jnp.int32, (n_ex, tokens), 0)
    named = (names == first) | (names == second)
    earlier = (lax.broadcasted_iota(jnp.int32, (tokens, tokens), 0)
               < lax.broadcasted_iota(jnp.int32, (tokens, tokens), 1))
    rank = jnp.dot(jnp.where(named, 1.0, 0.0).astype(BF16),
                   jnp.where(earlier, 1.0, 0.0).astype(BF16), preferred_element_type=F32)
    rank = jnp.where(named, rank.astype(jnp.int32), -1)
    scale_of = (jnp.where(names == first, weights_ref[0:1, :], 0.0)
                + jnp.where(names == second, weights_ref[1:2, :], 0.0))
    place = lax.broadcasted_iota(jnp.int32, (wide, tokens), 0)
    diagonal = (lax.broadcasted_iota(jnp.int32, (wide, LANES), 0)
                == lax.broadcasted_iota(jnp.int32, (wide, LANES), 1))
    picked = []
    for e in range(n_ex):
        chosen = place == rank[e:e + 1, :]
        picked.append(jnp.where(chosen, 1.0, 0.0))
        column = jnp.sum(jnp.where(chosen, scale_of[e:e + 1, :], 0.0), axis=1, keepdims=True)
        row = jnp.sum(jnp.where(diagonal, column, 0.0), axis=0, keepdims=True)
        scale_out[e] = jnp.broadcast_to(row, (8, LANES))

    pick[...] = jnp.concatenate(picked, axis=0).astype(BF16)
    pl.semaphore_wait(barrier, n_dp + n_ex - 2)

    def dispatch(c):
        rows = jnp.dot(pick[...], grad_ref[:, columns(c)], preferred_element_type=F32)
        send[c] = jnp.concatenate(
            [rows[:, :sub].reshape(n_ex, wide, sub), rows[:, sub:].reshape(n_ex, wide, sub)],
            axis=1).astype(BF16)
        each(1, n_ex, lambda k: row_copy(c, k).start())

        @pl.when(c == 0)
        def _():
            each(1, n_ex, lambda k: small_copy(scale_out, scale_in, sca_s, sca_r, k).start())
            scale_in[ex] = scale_out[ex]
        for h in range(2):
            mat_start(2 * c + h)
    each(0, chunks, dispatch)

    def keep_own(c):
        recv[c, ex] = send[c, ex]
        for h in range(2):
            full[2 * c + h, dp] = shard_ref[:, narrow(2 * c + h)]
    each(0, chunks, keep_own)

    padded = hidden_ref[...].astype(F32)
    if wide > cap:
        padded = jnp.concatenate([padded, jnp.zeros((n_ex, wide - cap, ff), F32)], axis=1)
    hid[...] = padded.reshape(n_ex * wide, ff).T.astype(BF16)

    each(1, n_ex, lambda k: small_arrival(scale_out, scale_in, sca_s, sca_r, k).wait())

    def scale_column():
        return jnp.concatenate(
            [jnp.sum(jnp.where(diagonal, scale_in[j, 0:1, :], 0.0), axis=1, keepdims=True)
             for j in range(n_ex)], axis=0)

    def pass_on(c):
        for h in range(2):
            mat_forward(2 * c + h, h)
    each(0, chunks, pass_on)

    scale = scale_column()

    def work(c):
        each(1, n_ex, lambda k: row_arrival(c, k).wait())
        both = recv[c].astype(F32)
        halves = [both[:, h * wide:(h + 1) * wide].reshape(n_ex * wide, sub) for h in range(2)]
        for h in range(2):
            weighted = (scale * halves[h]).astype(BF16)
            share = jnp.dot(hid[...], weighted, preferred_element_type=F32)
            part[2 * c + h] = share.astype(BF16).reshape(n_dp, depth, sub)
            red_start(2 * c + h, h)
        product = jnp.zeros(unscaled.shape, F32)
        for h in range(2):
            mat_wait(2 * c + h, h)
            product += lax.dot_general(
                halves[h].astype(BF16), full[2 * c + h].reshape(n_dp * depth, sub),
                (((1,), (1,)), ((), ())), preferred_element_type=F32)

        @pl.when(c == 0)
        def _():
            unscaled[...] = product

        @pl.when(c > 0)
        def _():
            unscaled[...] += product
            for h in range(2):
                red_forward(2 * (c - 1) + h, h)
    each(0, chunks, work)

    for j in range(n_ex):
        block = unscaled[j * wide:j * wide + cap, :]
        term = jnp.sum(hidden_ref[j].astype(F32) * block, axis=1, keepdims=True)
        row = jnp.sum(jnp.where(diagonal[0:cap], term, 0.0), axis=0, keepdims=True)
        term_out[j] = jnp.broadcast_to(row, (8, LANES))
    each(1, n_ex, lambda k: small_copy(term_out, term_in, ter_s, ter_r, k).start())
    term_in[ex] = term_out[ex]
    for h in range(2):
        red_forward(2 * (chunks - 1) + h, h)

    for j in range(n_ex):
        hgrad_ref[j] = (scale[j * wide:j * wide + cap] * unscaled[j * wide:j * wide + cap, :]).astype(BF16)

    def reduce(c):
        for h in range(2):
            wgrad_ref[:, narrow(2 * c + h)] = red_finish(2 * c + h, h)
    each(0, chunks, reduce)

    each(1, n_ex, lambda k: small_arrival(term_out, term_in, ter_s, ter_r, k).wait())
    first_out = jnp.zeros((1, tokens), F32)
    second_out = jnp.zeros((1, tokens), F32)
    for e in range(n_ex):
        column = jnp.sum(jnp.where(diagonal, term_in[e, 0:1, :], 0.0), axis=1, keepdims=True)
        back = jnp.sum(jnp.where(place == rank[e:e + 1, :], column, 0.0), axis=0, keepdims=True)
        first_out += jnp.where(first == e, back, 0.0)
        second_out += jnp.where(second == e, back, 0.0)
    rgrad_ref[0:1, :] = first_out
    rgrad_ref[1:2, :] = second_out


def per_device(output_grad, routes, combine_weights, saved_hidden, down_weight):
    n_dp, n_ex = lax.axis_size("dp"), lax.axis_size("expert")
    tokens, features = output_grad.shape
    slots, ff = saved_hidden.shape
    cap = slots // n_ex
    wide = -(-cap // 8) * 8
    depth = down_weight.shape[1]
    chunks = 8
    sub = features // (2 * chunks)
    dma = pltpu.SemaphoreType.DMA
    hgrad, wgrad, rgrad = pl.pallas_call(
        functools.partial(kernel, n_dp, n_ex, chunks),
        out_shape=(
            jax.ShapeDtypeStruct((n_ex, cap, ff), BF16),
            jax.ShapeDtypeStruct((depth, features), F32),
            jax.ShapeDtypeStruct((2, tokens), F32),
        ),
        in_specs=[pl.BlockSpec(memory_space=pltpu.VMEM)] * 5,
        out_specs=[pl.BlockSpec(memory_space=pltpu.VMEM)] * 3,
        scratch_shapes=[
            pltpu.VMEM((n_ex * wide, tokens), BF16),
            pltpu.VMEM((chunks, n_ex, 2 * wide, sub), BF16),
            pltpu.VMEM((chunks, n_ex, 2 * wide, sub), BF16),
            pltpu.VMEM((2 * chunks, n_dp, depth, sub), BF16),
            pltpu.VMEM((n_ex, 8, LANES), F32),
            pltpu.VMEM((n_ex, 8, LANES), F32),
            pltpu.VMEM((n_ex, 8, LANES), F32),
            pltpu.VMEM((n_ex, 8, LANES), F32),
            pltpu.VMEM((ff, n_ex * wide), BF16),
            pltpu.VMEM((n_ex * wide, ff), F32),
            pltpu.VMEM((2 * chunks, n_dp, depth, sub), BF16),
            pltpu.VMEM((2 * chunks, n_dp, depth, sub), BF16),
            dma((chunks, n_ex)), dma((chunks, n_ex)),
            dma((2 * chunks, n_dp)), dma((2 * chunks, n_dp)),
            dma((n_ex,)), dma((n_ex,)), dma((n_ex,)), dma((n_ex,)),
            dma((2 * chunks, n_dp)), dma((2 * chunks, n_dp)),
        ],
        compiler_params=pltpu.CompilerParams(
            collective_id=0, has_side_effects=True, vmem_limit_bytes=36 * 2**20
        ),
        cost_estimate=pl.CostEstimate(
            flops=4 * slots * features * ff, bytes_accessed=8 * 2**20, transcendentals=0),
    )(
        output_grad, routes.T, combine_weights.T.astype(F32),
        saved_hidden.reshape(n_ex, cap, ff), down_weight[0],
    )
    return hgrad.reshape(slots, ff), wgrad[None], rgrad.T


def solution(mesh):
    return jax.shard_map(
        per_device,
        mesh=mesh,
        in_specs=(
            P(("dp", "expert"), None),
            P(("dp", "expert"), None),
            P(("dp", "expert"), None),
            P(("dp", "expert"), None),
            P("expert", "dp", None),
        ),
        out_specs=(P(("dp", "expert"), None), P("expert", "dp", None), P(("dp", "expert"), None)),
        check_vma=False,
    )
```

```python
import functools

import jax
import jax.numpy as jnp
from jax import lax
from jax.experimental import pallas as pl
from jax.experimental.pallas import tpu as pltpu
from jax.sharding import PartitionSpec as P

MESH = pl.DeviceIdType.MESH
F32 = jnp.float32
BF16 = jnp.bfloat16
LANES = 128


def kernel(
    n_dp, n_ex, chunks,
    grad_ref, routes_ref, weights_ref, hidden_ref, shard_ref,
    hgrad_ref, wgrad_ref, rgrad_ref,
    pick, send, recv, full, scale_out, scale_in, term_out, term_in,
    hid, unscaled, part, landed,
    row_s, row_r, mat_s, mat_r, sca_s, sca_r, ter_s, ter_r, red_s, red_r,
):
    dp, ex = lax.axis_index("dp"), lax.axis_index("expert")
    cap = hidden_ref.shape[1]
    wide = send.shape[2] // 2
    sub = send.shape[3]
    fc = 2 * sub
    depth = shard_ref.shape[0]
    tokens = grad_ref.shape[0]
    ff = hidden_ref.shape[2]

    def columns(c):
        return pl.ds(pl.multiple_of(c * fc, fc), fc)

    def dp_copy(src, dst, s, r, to):
        return pltpu.make_async_remote_copy(
            src_ref=src, dst_ref=dst, send_sem=s, recv_sem=r,
            device_id=(to, ex), device_id_type=MESH)

    def narrow(t):
        return pl.ds(pl.multiple_of(t * sub, sub), sub)

    square = n_dp == 4
    across = dp + 1 - 2 * lax.rem(dp, 2)
    along = lax.rem(dp + 2, n_dp)
    corner = lax.rem(across + 2, n_dp)
    near = (across, along)

    def mat_copy(t, to):
        return dp_copy(shard_ref.at[:, narrow(t)], full.at[t, dp], mat_s.at[t, to], mat_r.at[t, dp], to)

    def mat_pass(t, h):
        return dp_copy(full.at[t, near[h]], full.at[t, near[h]], mat_s.at[t, corner],
                       mat_r.at[t, near[h]], near[1 - h])

    def mat_arrival(t, src):
        return dp_copy(shard_ref.at[:, narrow(t)], full.at[t, src], mat_s.at[t, src], mat_r.at[t, src], src)

    def mat_start(t):
        if square:
            mat_copy(t, across).start()
            mat_copy(t, along).start()
        else:
            each(1, n_dp, lambda k: mat_copy(t, lax.rem(dp + k, n_dp)).start())

    def mat_forward(t, h):
        if square:
            mat_arrival(t, near[h]).wait_recv()
            mat_pass(t, h).start()

    def mat_wait(t, h):
        if square:
            mat_arrival(t, near[1 - h]).wait_recv()
            mat_arrival(t, corner).wait()
            mat_arrival(t, across).wait_send()
            mat_arrival(t, along).wait_send()
        else:
            each(1, n_dp, lambda k: mat_arrival(t, lax.rem(dp + k, n_dp)).wait())

    def red_copy(t, block, slot, to):
        return dp_copy(part.at[t, block], landed.at[t, slot], red_s.at[t, slot], red_r.at[t, slot], to)

    def red_far(t, k):
        to = lax.rem(dp + k, n_dp)
        return dp_copy(part.at[t, to], landed.at[t, dp], red_s.at[t, to], red_r.at[t, dp], to)

    def red_far_arrival(t, k):
        src = lax.rem(dp + k, n_dp)
        return dp_copy(part.at[t, src], landed.at[t, src], red_s.at[t, src], red_r.at[t, src], src)

    def red_start(t, h):
        if square:
            red_copy(t, corner, 1, near[h]).start()
            red_copy(t, near[h], 0, near[h]).start()
        else:
            each(1, n_dp, lambda k: red_far(t, k).start())

    def red_forward(t, h):
        if square:
            red_copy(t, corner, 1, near[h]).wait()
            total = part[t, near[1 - h]].astype(F32) + landed[t, 1].astype(F32)
            part[t, near[1 - h]] = total.astype(BF16)
            red_copy(t, near[1 - h], 2, near[1 - h]).start()

    def red_finish(t, h):
        if square:
            red_copy(t, near[h], 0, near[h]).wait()
            red_copy(t, near[1 - h], 2, near[1 - h]).wait()
            return part[t, dp].astype(F32) + landed[t, 0].astype(F32) + landed[t, 2].astype(F32)
        each(1, n_dp, lambda k: red_far_arrival(t, k).wait())
        landed[t, dp] = part[t, dp]
        return jnp.sum(landed[t].astype(F32), axis=0)

    def row_copy(c, k):
        to = lax.rem(ex + k, n_ex)
        return pltpu.make_async_remote_copy(
            src_ref=send.at[c, to], dst_ref=recv.at[c, ex],
            send_sem=row_s.at[c, to], recv_sem=row_r.at[c, ex],
            device_id=(dp, to), device_id_type=MESH)

    def row_arrival(c, k):
        src = lax.rem(ex + k, n_ex)
        return pltpu.make_async_remote_copy(
            src_ref=send.at[c, src], dst_ref=recv.at[c, src],
            send_sem=row_s.at[c, src], recv_sem=row_r.at[c, src],
            device_id=(dp, src), device_id_type=MESH)

    def small_copy(out, into, s, r, k):
        to = lax.rem(ex + k, n_ex)
        return pltpu.make_async_remote_copy(
            src_ref=out.at[to], dst_ref=into.at[ex],
            send_sem=s.at[to], recv_sem=r.at[ex],
            device_id=(dp, to), device_id_type=MESH)

    def small_arrival(out, into, s, r, k):
        src = lax.rem(ex + k, n_ex)
        return pltpu.make_async_remote_copy(
            src_ref=out.at[src], dst_ref=into.at[src],
            send_sem=s.at[src], recv_sem=r.at[src],
            device_id=(dp, src), device_id_type=MESH)

    def each(low, high, body):
        def step(i, carry):
            body(i)
            return carry
        lax.fori_loop(low, high, step, 0)

    barrier = pltpu.get_barrier_semaphore()
    each(1, n_dp, lambda k: pl.semaphore_signal(
        barrier, inc=1, device_id=(lax.rem(dp + k, n_dp), ex), device_id_type=MESH))
    each(1, n_ex, lambda k: pl.semaphore_signal(
        barrier, inc=1, device_id=(dp, lax.rem(ex + k, n_ex)), device_id_type=MESH))

    first, second = routes_ref[0:1, :], routes_ref[1:2, :]
    names = lax.broadcasted_iota(jnp.int32, (n_ex, tokens), 0)
    named = (names == first) | (names == second)
    earlier = (lax.broadcasted_iota(jnp.int32, (tokens, tokens), 0)
               < lax.broadcasted_iota(jnp.int32, (tokens, tokens), 1))
    rank = jnp.dot(jnp.where(named, 1.0, 0.0).astype(BF16),
                   jnp.where(earlier, 1.0, 0.0).astype(BF16), preferred_element_type=F32)
    rank = jnp.where(named, rank.astype(jnp.int32), -1)
    scale_of = (jnp.where(names == first, weights_ref[0:1, :], 0.0)
                + jnp.where(names == second, weights_ref[1:2, :], 0.0))
    place = lax.broadcasted_iota(jnp.int32, (wide, tokens), 0)
    diagonal = (lax.broadcasted_iota(jnp.int32, (wide, LANES), 0)
                == lax.broadcasted_iota(jnp.int32, (wide, LANES), 1))
    picked = []
    for e in range(n_ex):
        chosen = place == rank[e:e + 1, :]
        picked.append(jnp.where(chosen, 1.0, 0.0))
        column = jnp.sum(jnp.where(chosen, scale_of[e:e + 1, :], 0.0), axis=1, keepdims=True)
        row = jnp.sum(jnp.where(diagonal, column, 0.0), axis=0, keepdims=True)
        scale_out[e] = jnp.broadcast_to(row, (8, LANES))

    pick[...] = jnp.concatenate(picked, axis=0).astype(BF16)
    pl.semaphore_wait(barrier, n_dp + n_ex - 2)

    def dispatch(c):
        rows = jnp.dot(pick[...], grad_ref[:, columns(c)], preferred_element_type=F32)
        send[c] = jnp.concatenate(
            [rows[:, :sub].reshape(n_ex, wide, sub), rows[:, sub:].reshape(n_ex, wide, sub)],
            axis=1).astype(BF16)
        each(1, n_ex, lambda k: row_copy(c, k).start())

        @pl.when(c == 0)
        def _():
            each(1, n_ex, lambda k: small_copy(scale_out, scale_in, sca_s, sca_r, k).start())
            scale_in[ex] = scale_out[ex]
        for h in range(2):
            mat_start(2 * c + h)
    each(0, chunks, dispatch)

    def keep_own(c):
        recv[c, ex] = send[c, ex]
        for h in range(2):
            full[2 * c + h, dp] = shard_ref[:, narrow(2 * c + h)]
    each(0, chunks, keep_own)

    padded = hidden_ref[...].astype(F32)
    if wide > cap:
        padded = jnp.concatenate([padded, jnp.zeros((n_ex, wide - cap, ff), F32)], axis=1)
    hid[...] = padded.reshape(n_ex * wide, ff).T.astype(BF16)

    each(1, n_ex, lambda k: small_arrival(scale_out, scale_in, sca_s, sca_r, k).wait())

    def scale_column():
        return jnp.concatenate(
            [jnp.sum(jnp.where(diagonal, scale_in[j, 0:1, :], 0.0), axis=1, keepdims=True)
             for j in range(n_ex)], axis=0)

    def pass_on(c):
        for h in range(2):
            mat_forward(2 * c + h, h)
    each(0, chunks, pass_on)

    scale = scale_column()

    def work(c):
        each(1, n_ex, lambda k: row_arrival(c, k).wait())
        both = recv[c].astype(F32)
        halves = [both[:, h * wide:(h + 1) * wide].reshape(n_ex * wide, sub) for h in range(2)]
        for h in range(2):
            weighted = (scale * halves[h]).astype(BF16)
            share = jnp.dot(hid[...], weighted, preferred_element_type=F32)
            part[2 * c + h] = share.astype(BF16).reshape(n_dp, depth, sub)
            red_start(2 * c + h, h)
        for h in range(2):
            mat_wait(2 * c + h, h)
        product = lax.dot_general(
            jnp.concatenate(halves, axis=1).astype(BF16),
            jnp.concatenate([full[2 * c + h].reshape(n_dp * depth, sub) for h in range(2)], axis=1),
            (((1,), (1,)), ((), ())), preferred_element_type=F32)

        @pl.when(c == 0)
        def _():
            unscaled[...] = product

        @pl.when(c > 0)
        def _():
            unscaled[...] += product
            for h in range(2):
                red_forward(2 * (c - 1) + h, h)
    each(0, chunks, work)

    for j in range(n_ex):
        block = unscaled[j * wide:j * wide + cap, :]
        term = jnp.sum(hidden_ref[j].astype(F32) * block, axis=1, keepdims=True)
        row = jnp.sum(jnp.where(diagonal[0:cap], term, 0.0), axis=0, keepdims=True)
        term_out[j] = jnp.broadcast_to(row, (8, LANES))
    each(1, n_ex, lambda k: small_copy(term_out, term_in, ter_s, ter_r, k).start())
    term_in[ex] = term_out[ex]
    for h in range(2):
        red_forward(2 * (chunks - 1) + h, h)

    for j in range(n_ex):
        hgrad_ref[j] = (scale[j * wide:j * wide + cap] * unscaled[j * wide:j * wide + cap, :]).astype(BF16)

    def reduce(c):
        for h in range(2):
            wgrad_ref[:, narrow(2 * c + h)] = red_finish(2 * c + h, h)
    each(0, chunks, reduce)

    each(1, n_ex, lambda k: small_arrival(term_out, term_in, ter_s, ter_r, k).wait())
    first_out = jnp.zeros((1, tokens), F32)
    second_out = jnp.zeros((1, tokens), F32)
    for e in range(n_ex):
        column = jnp.sum(jnp.where(diagonal, term_in[e, 0:1, :], 0.0), axis=1, keepdims=True)
        back = jnp.sum(jnp.where(place == rank[e:e + 1, :], column, 0.0), axis=0, keepdims=True)
        first_out += jnp.where(first == e, back, 0.0)
        second_out += jnp.where(second == e, back, 0.0)
    rgrad_ref[0:1, :] = first_out
    rgrad_ref[1:2, :] = second_out


def per_device(output_grad, routes, combine_weights, saved_hidden, down_weight):
    n_dp, n_ex = lax.axis_size("dp"), lax.axis_size("expert")
    tokens, features = output_grad.shape
    slots, ff = saved_hidden.shape
    cap = slots // n_ex
    wide = -(-cap // 8) * 8
    depth = down_weight.shape[1]
    chunks = 8
    sub = features // (2 * chunks)
    dma = pltpu.SemaphoreType.DMA
    hgrad, wgrad, rgrad = pl.pallas_call(
        functools.partial(kernel, n_dp, n_ex, chunks),
        out_shape=(
            jax.ShapeDtypeStruct((n_ex, cap, ff), BF16),
            jax.ShapeDtypeStruct((depth, features), F32),
            jax.ShapeDtypeStruct((2, tokens), F32),
        ),
        in_specs=[pl.BlockSpec(memory_space=pltpu.VMEM)] * 5,
        out_specs=[pl.BlockSpec(memory_space=pltpu.VMEM)] * 3,
        scratch_shapes=[
            pltpu.VMEM((n_ex * wide, tokens), BF16),
            pltpu.VMEM((chunks, n_ex, 2 * wide, sub), BF16),
            pltpu.VMEM((chunks, n_ex, 2 * wide, sub), BF16),
            pltpu.VMEM((2 * chunks, n_dp, depth, sub), BF16),
            pltpu.VMEM((n_ex, 8, LANES), F32),
            pltpu.VMEM((n_ex, 8, LANES), F32),
            pltpu.VMEM((n_ex, 8, LANES), F32),
            pltpu.VMEM((n_ex, 8, LANES), F32),
            pltpu.VMEM((ff, n_ex * wide), BF16),
            pltpu.VMEM((n_ex * wide, ff), F32),
            pltpu.VMEM((2 * chunks, n_dp, depth, sub), BF16),
            pltpu.VMEM((2 * chunks, n_dp, depth, sub), BF16),
            dma((chunks, n_ex)), dma((chunks, n_ex)),
            dma((2 * chunks, n_dp)), dma((2 * chunks, n_dp)),
            dma((n_ex,)), dma((n_ex,)), dma((n_ex,)), dma((n_ex,)),
            dma((2 * chunks, n_dp)), dma((2 * chunks, n_dp)),
        ],
        compiler_params=pltpu.CompilerParams(
            collective_id=0, has_side_effects=True, vmem_limit_bytes=36 * 2**20
        ),
        cost_estimate=pl.CostEstimate(
            flops=4 * slots * features * ff, bytes_accessed=8 * 2**20, transcendentals=0),
    )(
        output_grad, routes.T, combine_weights.T.astype(F32),
        saved_hidden.reshape(n_ex, cap, ff), down_weight[0],
    )
    return hgrad.reshape(slots, ff), wgrad[None], rgrad.T


def solution(mesh):
    return jax.shard_map(
        per_device,
        mesh=mesh,
        in_specs=(
            P(("dp", "expert"), None),
            P(("dp", "expert"), None),
            P(("dp", "expert"), None),
            P(("dp", "expert"), None),
            P("expert", "dp", None),
        ),
        out_specs=(P(("dp", "expert"), None), P("expert", "dp", None), P(("dp", "expert"), None)),
        check_vma=False,
    )
```
